256 devices in a mesh: dp: 4 (over y_lo, core), seq: 64 (over x, z, y_hi).
Axes of the slice: x: 4, y: 4 (y_hi: 2, y_lo: 2; y = y_hi * 2 + y_lo), z: 8, core: 2. Of those that a mesh axis runs over, the one named last changes fastest.
Arguments:
- inputs: bfloat16 [4, 32768, 1024], P('dp', 'seq'), may hold values from -24 to 24
- w_query: bfloat16 [1024, 1024], replicated, may hold values from -0.1875 to 0.1875
- w_key: bfloat16 [1024, 1024], replicated, may hold values from -0.1875 to 0.1875
- w_value: bfloat16 [1024, 1024], replicated, may hold values from -0.1875 to 0.1875
- key_proj: bfloat16 [256, 32768], P(None, 'seq'), may hold values from -6 to 6
- value_proj: bfloat16 [256, 32768], P(None, 'seq'), may hold values from -6 to 6
- cotangent: bfloat16 [4, 32768, 1024], P('dp', 'seq'), may hold values from -6 to 6
Outputs:
- attended: bfloat16 [4, 32768, 1024], P('dp', 'seq')
- grad_inputs: bfloat16 [4, 32768, 1024], P('dp', 'seq')
- grad_query: float32 [1024, 1024], P('seq')
- grad_key: float32 [1024, 1024], P('seq')
- grad_value: float32 [1024, 1024], P('seq')
The draws below stay inside these ranges and needn't reach their ends.
All inputs are finite; a program needn't handle non-finite values.
Results may differ from the reference program's by a relative error of at most 0.017.
The reference program's roundings to bfloat16 on the way (of `probs_low`, `dscore` and `dquery`) count: a program that leaves them out, or rounds other values in their place, can miss the bound.
Values sent between devices are 32-bit elements; how exact they have to be, the bound alone decides.
No kernel may reach another device: no remote copies, remote signals or barrier semaphores. Data moves between devices by JAX's collectives and lax.ppermute only.
A program may use at most 128 MiB of HBM per device.

```python
import math
import jax
import jax.numpy as jnp
from jax import lax

D = 1024
HEADS = 16
HEAD_DIM = 64
KP = 256
LENGTH = 32768
BATCH = 4


def draw_inputs(key, part):
    key = jax.random.fold_in(key, 11)
    noise_key = jax.random.fold_in(key, 0)
    values = jnp.clip(jax.random.normal(noise_key, (BATCH, LENGTH, D), jnp.float32), -6.0, 6.0)
    return values.astype(jnp.bfloat16)


def level_of(key, shape, cuts, smallest, high):
    loudness = 1.0
    for position, blocks in cuts:
        heights = jax.random.uniform(jax.random.fold_in(jax.random.fold_in(key, 6), position), (blocks,), jnp.float32, smallest / len(cuts), high / len(cuts))
        loudness = loudness * jnp.repeat(jnp.exp(heights), shape[position] // blocks).reshape((-1,) + (1,) * (len(shape) - 1 - position))
    return loudness


def bell_draw(stream_key, dims, deviation, limit, shards=(), dtype=jnp.bfloat16):
    values = deviation * jax.random.normal(stream_key, dims, jnp.float32)
    if shards:
        values = values * level_of(stream_key, dims, shards, -0.22, 0.18)
    return jnp.clip(values, -limit, limit).astype(dtype)


def setup_inputs(seed: int = 0) -> dict:
    streams_of = jax.random.split(jax.random.key(seed), 8)
    inputs = draw_inputs(jax.random.fold_in(streams_of[7], 71), 0)
    w_query = bell_draw(streams_of[1], (D, D), D ** -0.5, 0.1875)
    w_key = bell_draw(streams_of[2], (D, D), D ** -0.5, 0.1875)
    w_value = bell_draw(streams_of[3], (D, D), D ** -0.5, 0.1875)
    key_proj = bell_draw(streams_of[4], (KP, LENGTH), 1.0, 6.0, ((1, 64),))
    value_proj = bell_draw(streams_of[5], (KP, LENGTH), 1.0, 6.0, ((1, 64),))
    cotangent = bell_draw(streams_of[6], (BATCH, LENGTH, D), 1.0, 6.0, ((0, 4), (1, 64)))
    return {"inputs": inputs, "w_query": w_query, "w_key": w_key, "w_value": w_value, "key_proj": key_proj, "value_proj": value_proj, "cotangent": cotangent}


def rounded(value):
    return lax.optimization_barrier(value.astype(jnp.bfloat16)).astype(jnp.float32)

def one_document(weights, tokens, upstream):
    w_query, w_key, w_value, key_proj, value_proj = weights
    length = tokens.shape[0]
    scale = 1.0 / math.sqrt(HEAD_DIM)
    norm = 1.0 / math.sqrt(LENGTH)
    query = jnp.dot(tokens, w_query, preferred_element_type=jnp.float32).astype(jnp.bfloat16)
    keys = jnp.dot(tokens, w_key, preferred_element_type=jnp.float32).astype(jnp.bfloat16)
    values = jnp.dot(tokens, w_value, preferred_element_type=jnp.float32).astype(jnp.bfloat16)
    key_low = (jnp.dot(key_proj, keys, preferred_element_type=jnp.float32) * norm).astype(jnp.bfloat16)
    value_low = (jnp.dot(value_proj, values, preferred_element_type=jnp.float32) * norm).astype(jnp.bfloat16)
    query_h = query.astype(jnp.float32).reshape(length, HEADS, HEAD_DIM)
    key_h = key_low.astype(jnp.float32).reshape(KP, HEADS, HEAD_DIM)
    value_h = value_low.astype(jnp.float32).reshape(KP, HEADS, HEAD_DIM)
    upstream_h = upstream.astype(jnp.float32).reshape(length, HEADS, HEAD_DIM)
    scores = jnp.einsum('lhe,jhe->hlj', query_h, key_h) * scale
    probs = jax.nn.softmax(scores, axis=-1)
    probs_low = rounded(probs)
    attended = jnp.einsum('hlj,jhe->lhe', probs_low, value_h).reshape(length, D).astype(jnp.bfloat16)
    dprob = jnp.einsum('lhe,jhe->hlj', upstream_h, value_h)
    dscore = rounded(probs * (dprob - lax.optimization_barrier(jnp.sum(probs * dprob, axis=-1, keepdims=True))) * scale)
    dquery = jnp.einsum('hlj,jhe->lhe', dscore, key_h).reshape(length, D).astype(jnp.bfloat16)
    dkp = (jnp.einsum('hlj,lhe->jhe', dscore, query_h).reshape(KP, D) * norm).astype(jnp.bfloat16)
    dvp = (jnp.einsum('hlj,lhe->jhe', probs_low, upstream_h).reshape(KP, D) * norm).astype(jnp.bfloat16)
    dkeys = jnp.dot(key_proj.T, dkp, preferred_element_type=jnp.float32).astype(jnp.bfloat16)
    dvalues = jnp.dot(value_proj.T, dvp, preferred_element_type=jnp.float32).astype(jnp.bfloat16)
    grad_in = jnp.dot(dquery, w_query.T, preferred_element_type=jnp.float32)
    grad_in = grad_in + jnp.dot(dkeys, w_key.T, preferred_element_type=jnp.float32)
    grad_in = grad_in + jnp.dot(dvalues, w_value.T, preferred_element_type=jnp.float32)
    grad_q = jnp.dot(tokens.T, dquery, preferred_element_type=jnp.float32)
    grad_k = jnp.dot(tokens.T, dkeys, preferred_element_type=jnp.float32)
    grad_v = jnp.dot(tokens.T, dvalues, preferred_element_type=jnp.float32)
    return (attended, grad_in.astype(jnp.bfloat16), grad_q, grad_k, grad_v)

def reference(inputs, w_query, w_key, w_value, key_proj, value_proj, cotangent):
    weights = (w_query, w_key, w_value, key_proj, value_proj)

    def step(carry, pair):
        attended, grad_in, grad_q, grad_k, grad_v = one_document(weights, pair[0], pair[1])
        return ((carry[0] + grad_q, carry[1] + grad_k, carry[2] + grad_v), (attended, grad_in))
    start = jnp.zeros((D, D), jnp.float32)
    totals, outs = lax.scan(step, (start, start, start), (inputs, cotangent))
    factor = 1.0 / math.sqrt(BATCH * LENGTH)
    return (outs[0], outs[1], totals[0] * factor, totals[1] * factor, totals[2] * factor)
```

```python
import math

import jax
import jax.numpy as jnp
from jax import lax
from jax.sharding import Mesh
from jax.sharding import PartitionSpec as P

HEADS = 16
SPLITS = {64: (4, 8, 2), 8: (2, 2, 2)}
SEQ = ("x", "z", "yh")


def bf16_dot(spec, a, b):
    return jnp.einsum(spec, a, b, preferred_element_type=jnp.float32)


def scatter_sum(part):
    rows, width = part.shape
    plane = lax.axis_size(("x", "yh"))
    depth = lax.axis_size("z")
    got = lax.all_to_all(part.reshape(plane, rows // plane, width), ("x", "yh"), 0, 0)
    mine = jnp.sum(got, axis=0)
    got = lax.all_to_all(mine.reshape(depth, rows // plane // depth, width), "z", 0, 0)
    return jnp.sum(got, axis=0)


def gather_rows(mine):
    rows, width = mine.shape
    plane = lax.axis_size(("x", "yh"))
    depth = lax.axis_size("z")
    got = lax.all_to_all(jnp.broadcast_to(mine, (depth, rows, width)), "z", 0, 0)
    got = got.reshape(depth * rows, width)
    got = lax.all_to_all(jnp.broadcast_to(got, (plane, depth * rows, width)), ("x", "yh"), 0, 0)
    return got.reshape(plane * depth * rows, width)


def by_z(part):
    rows, width = part.shape
    n_x, n_z, n_yh = (lax.axis_size(a) for a in SEQ)
    block = rows // (n_x * n_z * n_yh)
    part = part.reshape(n_x, n_z, n_yh * block, width)
    return jnp.swapaxes(part, 0, 1).reshape(rows, width)


def scatter_rows(part, axes):
    for axis in axes:
        part = lax.psum_scatter(part, axis, scatter_dimension=0, tiled=True)
    return part


def pair_sum(part, axis):
    return part + lax.ppermute(part, axis, [(0, 1), (1, 0)])


def body(inputs, w_query, w_key, w_value, key_proj, value_proj, cotangent):
    inputs, cotangent = inputs[0], cotangent[0]
    rows, width = inputs.shape
    head_dim = width // HEADS
    proj_rows = key_proj.shape[0]
    scale = 1.0 / math.sqrt(head_dim)
    n_seq = lax.axis_size(SEQ)
    n_data = lax.axis_size(("yl", "core"))
    norm = 1.0 / math.sqrt(rows * n_seq)
    factor = 1.0 / math.sqrt(rows * n_seq * n_data)

    keys = bf16_dot("lc,cd->ld", inputs, w_key).astype(jnp.bfloat16)
    values = bf16_dot("lc,cd->ld", inputs, w_value).astype(jnp.bfloat16)
    key_part = bf16_dot("jl,ld->jd", key_proj, keys)
    value_part = bf16_dot("jl,ld->jd", value_proj, values)
    sums = gather_rows(scatter_sum(jnp.concatenate([key_part, value_part], axis=0)))

    both_proj = jnp.concatenate([key_proj, value_proj], axis=0)
    seen = by_z(bf16_dot("lc,jl->cj", inputs, both_proj))
    seen = scatter_rows(seen, ("z", "x", "yh"))

    query = bf16_dot("lc,cd->ld", inputs, w_query).astype(jnp.bfloat16)
    low = (sums * norm).astype(jnp.bfloat16)
    key_h = low[:proj_rows].reshape(proj_rows, HEADS, head_dim)
    value_h = low[proj_rows:].reshape(proj_rows, HEADS, head_dim)
    query_h = query.reshape(rows, HEADS, head_dim)
    upstream_h = cotangent.reshape(rows, HEADS, head_dim)
    scores = bf16_dot("lhe,jhe->hlj", query_h, key_h) * scale
    probs = jax.nn.softmax(scores, axis=-1)
    probs_low = probs.astype(jnp.bfloat16)
    attended = bf16_dot("hlj,jhe->lhe", probs_low, value_h)
    attended = attended.reshape(rows, width).astype(jnp.bfloat16)
    dprob = bf16_dot("lhe,jhe->hlj", upstream_h, value_h)
    dscore = (probs * (dprob - jnp.sum(probs * dprob, axis=-1, keepdims=True)) * scale).astype(
        jnp.bfloat16
    )
    dquery = bf16_dot("hlj,jhe->lhe", dscore, key_h).reshape(rows, width).astype(jnp.bfloat16)
    dkp_part = bf16_dot("hlj,lhe->jhe", dscore, query_h).reshape(proj_rows, width)
    dvp_part = bf16_dot("hlj,lhe->jhe", probs_low, upstream_h).reshape(proj_rows, width)

    dquery_blocks = dquery.reshape(rows, n_data, width // n_data)
    grad_q = jnp.stack(
        [bf16_dot("lc,ld->cd", inputs, dquery_blocks[:, p]) for p in range(n_data)]
    )
    grad_q = grad_q.reshape(2, 2 * width, width // n_data)
    grad_q = jnp.sum(lax.all_to_all(grad_q, "core", 0, 0), axis=0)
    grad_q = jnp.concatenate([by_z(grad_q[:width]), by_z(grad_q[width:])], axis=1)
    grad_q = scatter_rows(grad_q, ("z", "x", "yh"))
    grad_q = jnp.stack([grad_q[:, : width // n_data], grad_q[:, width // n_data :]])
    grad_q = lax.psum_scatter(grad_q, "yl", scatter_dimension=0)

    sums = gather_rows(scatter_sum(jnp.concatenate([dkp_part, dvp_part], axis=0)))
    low = (sums * norm).astype(jnp.bfloat16)
    dkp_low, dvp_low = low[:proj_rows], low[proj_rows:]
    seen_high = seen.astype(jnp.bfloat16)
    seen_low = (seen - seen_high.astype(jnp.float32)).astype(jnp.bfloat16)
    grad_k = bf16_dot("cj,jd->cd", seen_high[:, :proj_rows], dkp_low)
    grad_k = grad_k + bf16_dot("cj,jd->cd", seen_low[:, :proj_rows], dkp_low)
    grad_v = bf16_dot("cj,jd->cd", seen_high[:, proj_rows:], dvp_low)
    grad_v = grad_v + bf16_dot("cj,jd->cd", seen_low[:, proj_rows:], dvp_low)
    place = lax.axis_index("core") * 2 + lax.axis_index("yl")
    column = lax.broadcasted_iota(jnp.int32, (1, n_data, 1), 1)
    grad_q = jnp.where(column == place, grad_q[:, None, :], 0.0).reshape(-1, width)
    grads = jnp.concatenate([grad_q, grad_k, grad_v], axis=0) * factor
    grads = pair_sum(pair_sum(grads, "core"), "yl")
    grad_q, grad_k, grad_v = jnp.split(grads, 3, axis=0)

    dkeys = bf16_dot("jl,jd->ld", key_proj, dkp_low).astype(jnp.bfloat16)
    dvalues = bf16_dot("jl,jd->ld", value_proj, dvp_low).astype(jnp.bfloat16)
    grad_in = bf16_dot("ld,cd->lc", dquery, w_query)
    grad_in = grad_in + bf16_dot("ld,cd->lc", dkeys, w_key)
    grad_in = grad_in + bf16_dot("ld,cd->lc", dvalues, w_value)
    grad_inputs = grad_in.astype(jnp.bfloat16)
    return (attended[None], grad_inputs[None], grad_q, grad_k, grad_v)


def solution(mesh):
    split = SPLITS[mesh.shape["seq"]]
    fine = Mesh(mesh.devices.reshape((2, 2) + split), ("yl", "core") + SEQ)
    tokens = P(("yl", "core"), SEQ, None)
    return jax.shard_map(
        body,
        mesh=fine,
        in_specs=(tokens, P(), P(), P(), P(None, SEQ), P(None, SEQ), tokens),
        out_specs=(tokens, tokens, P(SEQ, None), P(SEQ, None), P(SEQ, None)),
        check_vma=False,
    )
```

```python
import functools
import math

import jax
import jax.numpy as jnp
from jax import lax
from jax.experimental import pallas as pl
from jax.experimental.pallas import tpu as pltpu
from jax.sharding import Mesh
from jax.sharding import PartitionSpec as P

HEADS = 16
HEAD_DIM = 64
SPLITS = {64: (4, 8, 2), 8: (4, 2, 1)}
SEQ = ("x", "z", "yh")
VMEM_LIMIT = 40 * 1024 * 1024


def dot(a, b):
    return jnp.dot(a, b, preferred_element_type=jnp.float32)


def dot_t(a, b):
    return lax.dot_general(a, b, (((1,), (1,)), ((), ())), preferred_element_type=jnp.float32)


def project_kernel(x_ref, wq_ref, wk_ref, wv_ref, kproj_ref, vproj_ref, query_ref, part_ref, xt_ref, seen_ref):
    width = query_ref.shape[1]
    proj = kproj_ref.shape[0]
    x = x_ref[...]
    kproj, vproj = kproj_ref[...], vproj_ref[...]
    columns = pl.ds(pl.multiple_of(pl.program_id(0) * width, width), width)
    xt = x_ref[:, columns].T
    xt_ref[...] = xt
    n_z, _, chunk, _ = seen_ref.shape
    seen_ref[:, 0, :, :proj] = dot_t(xt, kproj).reshape(n_z, chunk, proj)
    seen_ref[:, 0, :, proj:] = dot_t(xt, vproj).reshape(n_z, chunk, proj)
    part_ref[:proj] = dot(kproj, dot(x, wk_ref[...]).astype(jnp.bfloat16))
    part_ref[proj:] = dot(vproj, dot(x, wv_ref[...]).astype(jnp.bfloat16))
    query_ref[...] = dot(x, wq_ref[...]).astype(jnp.bfloat16)


def project(inputs, w_query, w_key, w_value, key_proj, value_proj):
    rows, width = inputs.shape
    proj = key_proj.shape[0]
    n_x, n_z = lax.axis_size("x"), lax.axis_size("z")
    block = width // n_x
    whole = lambda a: pl.BlockSpec(a.shape, lambda i: (0, 0))
    weight = pl.BlockSpec((width, block), lambda i: (0, i))
    return pl.pallas_call(
        project_kernel,
        grid=(n_x,),
        in_specs=[whole(inputs), weight, weight, weight, whole(key_proj), whole(value_proj)],
        out_specs=[
            pl.BlockSpec((rows, block), lambda i: (0, i)),
            pl.BlockSpec((2 * proj, block), lambda i: (0, i)),
            pl.BlockSpec((block, rows), lambda i: (i, 0)),
            pl.BlockSpec((n_z, 1, block // n_z, 2 * proj), lambda i: (0, i, 0, 0)),
        ],
        out_shape=[
            jax.ShapeDtypeStruct((rows, width), jnp.bfloat16),
            jax.ShapeDtypeStruct((2 * proj, width), jnp.float32),
            jax.ShapeDtypeStruct((width, rows), jnp.bfloat16),
            jax.ShapeDtypeStruct((n_z, n_x, block // n_z, 2 * proj), jnp.float32),
        ],
        compiler_params=pltpu.CompilerParams(vmem_limit_bytes=VMEM_LIMIT),
        cost_estimate=pl.CostEstimate(
            flops=2 * rows * width * (3 * width + 4 * proj), bytes_accessed=14 << 20, transcendentals=0
        ),
        name="project",
    )(inputs, w_query, w_key, w_value, key_proj, value_proj)


def attend_kernel(
    norm, core_ref, q_ref, c_ref, ks_ref, vs_ref, xt_ref, att_ref, dq_ref, dsum_ref, other_ref, mine_ref
):
    step = pl.program_id(0)
    proj, block = ks_ref.shape
    scale = 1.0 / math.sqrt(HEAD_DIM)
    q, c = q_ref[...], c_ref[...]
    qt, ct = q.T, c.T
    kp = (ks_ref[...] * norm).astype(jnp.bfloat16).astype(jnp.float32)
    vp = (vs_ref[...] * norm).astype(jnp.bfloat16).astype(jnp.float32)
    kpt, vpt = kp.T, vp.T
    lane = lax.broadcasted_iota(jnp.int32, (proj, block), 1)
    sub = lax.broadcasted_iota(jnp.int32, (block, proj), 0)
    att = dq = dk = dv = None
    for h in range(block // HEAD_DIM):
        in_lane = (lane >= h * HEAD_DIM) & (lane < (h + 1) * HEAD_DIM)
        in_sub = (sub >= h * HEAD_DIM) & (sub < (h + 1) * HEAD_DIM)
        one = lambda mask, v: jnp.where(mask, v, 0.0).astype(jnp.bfloat16)
        scores = dot(one(in_lane, kp * scale), qt)
        top = jnp.max(scores, axis=0, keepdims=True)
        probs = jnp.exp(scores - top)
        probs = probs * (1.0 / jnp.sum(probs, axis=0, keepdims=True))
        low = probs.astype(jnp.bfloat16)
        dprob = dot(one(in_lane, vp), ct)
        delta = jnp.sum(probs * dprob, axis=0, keepdims=True)
        dscore = (probs * (dprob - delta)).astype(jnp.bfloat16)
        att_h = dot(one(in_sub, vpt), low)
        dq_h = dot(one(in_sub, kpt), dscore)
        dk_h = dot(dscore, q)
        dv_h = dot(low, c)
        if h == 0:
            att, dq, dk, dv = att_h, dq_h, dk_h, dv_h
        else:
            att, dq = att + att_h, dq + dq_h
            dk, dv = jnp.where(in_lane, dk_h, dk), jnp.where(in_lane, dv_h, dv)
    att_ref[...] = att.T.astype(jnp.bfloat16)
    dquery = (dq * scale).T.astype(jnp.bfloat16)
    dq_ref[...] = dquery
    dsum_ref[:proj] = dk * scale
    dsum_ref[proj:] = dv

    def put(ref):
        n_z, n_x, _, chunk, _ = ref.shape
        for x in range(n_x):
            rows = n_z * chunk
            term = dot(xt_ref[x * rows : (x + 1) * rows], dquery)
            ref[:, x, 0] = term.reshape(n_z, chunk, block)

    pl.when(step < 2)(functools.partial(put, other_ref))
    pl.when(step >= 2)(functools.partial(put, mine_ref))


def attend(query, cotangent, sums, inputs_t, norm):
    rows, width = query.shape
    proj = sums.shape[0] // 2
    n_x, n_z = lax.axis_size("x"), lax.axis_size("z")
    block = width // 4
    core = lax.axis_index("core").astype(jnp.int32).reshape(1)
    place = lambda i, core: lax.rem(i + 2 * (1 - core[0]), 4)
    tokens = pl.BlockSpec((rows, block), lambda i, core: (0, place(i, core)))
    terms = (n_z, n_x, 2, width // (n_x * n_z), block)
    terms_block = (n_z, n_x, 1, width // (n_x * n_z), block)
    return pl.pallas_call(
        functools.partial(attend_kernel, norm),
        grid_spec=pltpu.PrefetchScalarGridSpec(
            num_scalar_prefetch=1,
            grid=(4,),
            in_specs=[
                tokens,
                tokens,
                pl.BlockSpec((proj, block), lambda i, core: (0, place(i, core))),
                pl.BlockSpec((proj, block), lambda i, core: (1, place(i, core))),
                pl.BlockSpec((width, rows), lambda i, core: (0, 0)),
            ],
            out_specs=[
                tokens,
                tokens,
                pl.BlockSpec((2 * proj, block), lambda i, core: (0, place(i, core))),
                pl.BlockSpec(terms_block, lambda i, core: (0, 0, jnp.minimum(i, 1), 0, 0)),
                pl.BlockSpec(terms_block, lambda i, core: (0, 0, jnp.maximum(i - 2, 0), 0, 0)),
            ],
        ),
        out_shape=[
            jax.ShapeDtypeStruct((rows, width), jnp.bfloat16),
            jax.ShapeDtypeStruct((rows, width), jnp.bfloat16),
            jax.ShapeDtypeStruct((2 * proj, width), jnp.float32),
            jax.ShapeDtypeStruct(terms, jnp.float32),
            jax.ShapeDtypeStruct(terms, jnp.float32),
        ],
        compiler_params=pltpu.CompilerParams(vmem_limit_bytes=VMEM_LIMIT),
        cost_estimate=pl.CostEstimate(
            flops=8 * rows * width * proj * 6, bytes_accessed=12 << 20, transcendentals=rows * HEADS * proj
        ),
        name="attend",
    )(core, query, cotangent, sums, sums, inputs_t)


def scatter_sum(part):
    rows, width = part.shape
    plane = lax.axis_size(("x", "yh"))
    depth = lax.axis_size("z")
    got = lax.all_to_all(part.reshape(plane, rows // plane, width), ("x", "yh"), 0, 0)
    mine = jnp.sum(got, axis=0)
    got = lax.all_to_all(mine.reshape(depth, rows // plane // depth, width), "z", 0, 0)
    return jnp.sum(got, axis=0)


def gather_rows(mine):
    rows, width = mine.shape
    plane = lax.axis_size(("x", "yh"))
    depth = lax.axis_size("z")
    got = lax.all_to_all(jnp.broadcast_to(mine, (depth, rows, width)), "z", 0, 0)
    got = got.reshape(depth * rows, width)
    got = lax.all_to_all(jnp.broadcast_to(got, (plane, depth * rows, width)), ("x", "yh"), 0, 0)
    return got.reshape(plane * depth * rows, width)


def scatter_rows(part, axes):
    for axis in axes:
        part = lax.psum_scatter(part, axis, scatter_dimension=0, tiled=True)
    return part


def keep_half(part, axis):
    if lax.axis_size(axis) == 1:
        return part.reshape((-1,) + part.shape[2:])
    me = lax.axis_index(axis)
    other = lax.dynamic_index_in_dim(part, 1 - me, 0, keepdims=False)
    mine = lax.dynamic_index_in_dim(part, me, 0, keepdims=False)
    return mine + lax.ppermute(other, axis, [(0, 1), (1, 0)])


def pair_sum(part, axis):
    return part + lax.ppermute(part, axis, [(0, 1), (1, 0)])


def body(inputs, w_query, w_key, w_value, key_proj, value_proj, cotangent):
    inputs, cotangent = inputs[0], cotangent[0]
    rows, width = inputs.shape
    proj = key_proj.shape[0]
    n_seq = lax.axis_size(SEQ)
    n_data = lax.axis_size(("yl", "core"))
    norm = 1.0 / math.sqrt(rows * n_seq)
    factor = 1.0 / math.sqrt(rows * n_seq * n_data)

    query, part, inputs_t, seen = project(inputs, w_query, w_key, w_value, key_proj, value_proj)
    seen = scatter_rows(seen.reshape(width, 2 * proj), ("z", "x"))
    seen = keep_half(seen.reshape(2, -1, 2 * proj), "yh")
    sums = gather_rows(scatter_sum(part))

    attended, dquery, part, other, mine = attend(query, cotangent, sums, inputs_t, norm)

    grad_q = mine + lax.ppermute(other, "core", [(0, 1), (1, 0)])
    grad_q = scatter_rows(grad_q.reshape(-1, width // n_data), ("z", "x"))
    grad_q = keep_half(grad_q.reshape(2, -1, width // n_data), "yl")
    grad_q = keep_half(grad_q.reshape(2, -1, width // n_data), "yh")

    sums = gather_rows(scatter_sum(part))
    low = (sums * norm).astype(jnp.bfloat16)
    dkp_low, dvp_low = low[:proj], low[proj:]
    seen_high = seen.astype(jnp.bfloat16)
    seen_low = (seen - seen_high.astype(jnp.float32)).astype(jnp.bfloat16)
    grad_k = dot(seen_high[:, :proj], dkp_low) + dot(seen_low[:, :proj], dkp_low)
    grad_v = dot(seen_high[:, proj:], dvp_low) + dot(seen_low[:, proj:], dvp_low)
    place = lax.axis_index("core") * 2 + lax.axis_index("yl")
    column = lax.broadcasted_iota(jnp.int32, (1, n_data, 1), 1)
    grad_q = jnp.where(column == place, grad_q[:, None, :], 0.0).reshape(-1, width)
    grads = jnp.concatenate([grad_q, grad_k, grad_v], axis=0) * factor
    grads = pair_sum(pair_sum(grads, "core"), "yl")
    grad_q, grad_k, grad_v = jnp.split(grads, 3, axis=0)

    dkeys = lax.dot_general(
        key_proj, dkp_low, (((0,), (0,)), ((), ())), preferred_element_type=jnp.float32
    ).astype(jnp.bfloat16)
    dvalues = lax.dot_general(
        value_proj, dvp_low, (((0,), (0,)), ((), ())), preferred_element_type=jnp.float32
    ).astype(jnp.bfloat16)
    grad_in = dot_t(dquery, w_query)
    grad_in = grad_in + dot_t(dkeys, w_key)
    grad_in = grad_in + dot_t(dvalues, w_value)
    grad_inputs = grad_in.astype(jnp.bfloat16)
    return (attended[None], grad_inputs[None], grad_q, grad_k, grad_v)


def solution(mesh):
    split = SPLITS[mesh.shape["seq"]]
    fine = Mesh(mesh.devices.reshape((2, 2) + split), ("yl", "core") + SEQ)
    tokens = P(("yl", "core"), SEQ, None)
    return jax.shard_map(
        body,
        mesh=fine,
        in_specs=(tokens, P(), P(), P(), P(None, SEQ), P(None, SEQ), tokens),
        out_specs=(tokens, tokens, P(SEQ, None), P(SEQ, None), P(SEQ, None)),
        check_vma=False,
    )
```

```python
import functools
import math

import jax
import jax.numpy as jnp
from jax import lax
from jax.experimental import pallas as pl
from jax.experimental.pallas import tpu as pltpu
from jax.sharding import Mesh
from jax.sharding import PartitionSpec as P

HEADS = 16
HEAD_DIM = 64
SPLITS = {64: (4, 4, 2, 2), 8: (4, 2, 1, 1)}
SEQ = ("x", "zh", "zl", "yh")
Z = ("zh", "zl")
NEAR = ("x", "zl", "yh")
VMEM_LIMIT = 60 * 1024 * 1024


def dot(a, b):
    return jnp.dot(a, b, preferred_element_type=jnp.float32)


def dot_t(a, b):
    return lax.dot_general(a, b, (((1,), (1,)), ((), ())), preferred_element_type=jnp.float32)


def project_kernel(x_ref, wq_ref, wk_ref, wv_ref, kproj_ref, vproj_ref, query_ref, part_ref, xt_ref, seen_ref):
    width = query_ref.shape[1]
    proj = kproj_ref.shape[0]
    x = x_ref[...]
    kproj, vproj = kproj_ref[...], vproj_ref[...]
    columns = pl.ds(pl.multiple_of(pl.program_id(0) * width, width), width)
    xt = x_ref[:, columns].T
    xt_ref[...] = xt
    n_z, _, chunk, _ = seen_ref.shape
    seen_ref[:, 0, :, :proj] = dot_t(xt, kproj).reshape(n_z, chunk, proj)
    seen_ref[:, 0, :, proj:] = dot_t(xt, vproj).reshape(n_z, chunk, proj)
    part_ref[:proj] = dot(kproj, dot(x, wk_ref[...]).astype(jnp.bfloat16))
    part_ref[proj:] = dot(vproj, dot(x, wv_ref[...]).astype(jnp.bfloat16))
    query_ref[...] = dot(x, wq_ref[...]).astype(jnp.bfloat16)


def project(inputs, w_query, w_key, w_value, key_proj, value_proj):
    rows, width = inputs.shape
    proj = key_proj.shape[0]
    n_x, n_z = lax.axis_size("x"), lax.axis_size(Z)
    block = width // n_x
    whole = lambda a: pl.BlockSpec(a.shape, lambda i: (0, 0))
    weight = pl.BlockSpec((width, block), lambda i: (0, i))
    return pl.pallas_call(
        project_kernel,
        grid=(n_x,),
        in_specs=[whole(inputs), weight, weight, weight, whole(key_proj), whole(value_proj)],
        out_specs=[
            pl.BlockSpec((rows, block), lambda i: (0, i)),
            pl.BlockSpec((2 * proj, block), lambda i: (0, i)),
            pl.BlockSpec((block, rows), lambda i: (i, 0)),
            pl.BlockSpec((n_z, 1, block // n_z, 2 * proj), lambda i: (0, i, 0, 0)),
        ],
        out_shape=[
            jax.ShapeDtypeStruct((rows, width), jnp.bfloat16),
            jax.ShapeDtypeStruct((2 * proj, width), jnp.float32),
            jax.ShapeDtypeStruct((width, rows), jnp.bfloat16),
            jax.ShapeDtypeStruct((n_z, n_x, block // n_z, 2 * proj), jnp.float32),
        ],
        compiler_params=pltpu.CompilerParams(vmem_limit_bytes=VMEM_LIMIT),
        cost_estimate=pl.CostEstimate(
            flops=2 * rows * width * (3 * width + 4 * proj), bytes_accessed=14 << 20, transcendentals=0
        ),
        name="project",
    )(inputs, w_query, w_key, w_value, key_proj, value_proj)


def attend_kernel(
    norm, core_ref, q_ref, c_ref, ks_ref, vs_ref, xt_ref, att_ref, dq_ref, dsum_ref, other_ref, mine_ref
):
    step = pl.program_id(0)
    proj, block = ks_ref.shape
    scale = 1.0 / math.sqrt(HEAD_DIM)
    q, c = q_ref[...], c_ref[...]
    qt, ct = q.T, c.T
    kp = (ks_ref[...] * norm).astype(jnp.bfloat16).astype(jnp.float32)
    vp = (vs_ref[...] * norm).astype(jnp.bfloat16).astype(jnp.float32)
    kpt, vpt = kp.T, vp.T
    lane = lax.broadcasted_iota(jnp.int32, (proj, block), 1)
    sub = lax.broadcasted_iota(jnp.int32, (block, proj), 0)
    att = dq = dk = dv = None
    for h in range(block // HEAD_DIM):
        in_lane = (lane >= h * HEAD_DIM) & (lane < (h + 1) * HEAD_DIM)
        in_sub = (sub >= h * HEAD_DIM) & (sub < (h + 1) * HEAD_DIM)
        one = lambda mask, v: jnp.where(mask, v, 0.0).astype(jnp.bfloat16)
        scores = dot(one(in_lane, kp * scale), qt)
        top = jnp.max(scores, axis=0, keepdims=True)
        probs = jnp.exp(scores - top)
        probs = probs * (1.0 / jnp.sum(probs, axis=0, keepdims=True))
        low = probs.astype(jnp.bfloat16)
        dprob = dot(one(in_lane, vp), ct)
        delta = jnp.sum(probs * dprob, axis=0, keepdims=True)
        dscore = (probs * (dprob - delta)).astype(jnp.bfloat16)
        att_h = dot(one(in_sub, vpt), low)
        dq_h = dot(one(in_sub, kpt), dscore)
        dk_h = dot(dscore, q)
        dv_h = dot(low, c)
        if h == 0:
            att, dq, dk, dv = att_h, dq_h, dk_h, dv_h
        else:
            att, dq = att + att_h, dq + dq_h
            dk, dv = jnp.where(in_lane, dk_h, dk), jnp.where(in_lane, dv_h, dv)
    att_ref[...] = att.T.astype(jnp.bfloat16)
    dquery = (dq * scale).T.astype(jnp.bfloat16)
    dq_ref[...] = dquery
    dsum_ref[:proj] = dk * scale
    dsum_ref[proj:] = dv

    def put(ref):
        n_z, n_x, _, chunk, _ = ref.shape
        for x in range(n_x):
            rows = n_z * chunk
            term = dot(xt_ref[x * rows : (x + 1) * rows], dquery)
            ref[:, x, 0] = term.reshape(n_z, chunk, block)

    pl.when(step < 2)(functools.partial(put, other_ref))
    pl.when(step >= 2)(functools.partial(put, mine_ref))


def attend(query, cotangent, sums, inputs_t, norm):
    rows, width = query.shape
    proj = sums.shape[0] // 2
    n_x, n_z = lax.axis_size("x"), lax.axis_size(Z)
    block = width // 4
    core = lax.axis_index("core").astype(jnp.int32).reshape(1)
    place = lambda i, core: lax.rem(i + 2 * (1 - core[0]), 4)
    tokens = pl.BlockSpec((rows, block), lambda i, core: (0, place(i, core)))
    terms = (n_z, n_x, 2, width // (n_x * n_z), block)
    terms_block = (n_z, n_x, 1, width // (n_x * n_z), block)
    return pl.pallas_call(
        functools.partial(attend_kernel, norm),
        grid_spec=pltpu.PrefetchScalarGridSpec(
            num_scalar_prefetch=1,
            grid=(4,),
            in_specs=[
                tokens,
                tokens,
                pl.BlockSpec((proj, block), lambda i, core: (0, place(i, core))),
                pl.BlockSpec((proj, block), lambda i, core: (1, place(i, core))),
                pl.BlockSpec((width, rows), lambda i, core: (0, 0)),
            ],
            out_specs=[
                tokens,
                tokens,
                pl.BlockSpec((2 * proj, block), lambda i, core: (0, place(i, core))),
                pl.BlockSpec(terms_block, lambda i, core: (0, 0, jnp.minimum(i, 1), 0, 0)),
                pl.BlockSpec(terms_block, lambda i, core: (0, 0, jnp.maximum(i - 2, 0), 0, 0)),
            ],
        ),
        out_shape=[
            jax.ShapeDtypeStruct((rows, width), jnp.bfloat16),
            jax.ShapeDtypeStruct((rows, width), jnp.bfloat16),
            jax.ShapeDtypeStruct((2 * proj, width), jnp.float32),
            jax.ShapeDtypeStruct(terms, jnp.float32),
            jax.ShapeDtypeStruct(terms, jnp.float32),
        ],
        compiler_params=pltpu.CompilerParams(vmem_limit_bytes=VMEM_LIMIT),
        cost_estimate=pl.CostEstimate(
            flops=8 * rows * width * proj * 6, bytes_accessed=12 << 20, transcendentals=rows * HEADS * proj
        ),
        name="attend",
    )(core, query, cotangent, sums, sums, inputs_t)


def input_grads_kernel(
    norm, sums_ref, dq_ref, kproj_ref, vproj_ref, wq_ref, wk_ref, wv_ref, out_ref, dkeys_ref, dvalues_ref
):
    proj = kproj_ref.shape[0]

    @pl.when(pl.program_id(0) == 0)
    def _():
        dkp = (sums_ref[:proj] * norm).astype(jnp.bfloat16)
        dkeys_ref[...] = dot(kproj_ref[...].T, dkp).astype(jnp.bfloat16)
        dvp = (sums_ref[proj:] * norm).astype(jnp.bfloat16)
        dvalues_ref[...] = dot(vproj_ref[...].T, dvp).astype(jnp.bfloat16)

    grad = dot_t(dq_ref[...], wq_ref[...]) + dot_t(dkeys_ref[...], wk_ref[...])
    out_ref[...] = (grad + dot_t(dvalues_ref[...], wv_ref[...])).astype(jnp.bfloat16)


def input_grads(sums, dquery, key_proj, value_proj, w_query, w_key, w_value, norm):
    rows, width = dquery.shape
    block = width // 4
    whole = lambda a: pl.BlockSpec(a.shape, lambda i: (0, 0))
    weight = pl.BlockSpec((block, width), lambda i: (i, 0))
    return pl.pallas_call(
        functools.partial(input_grads_kernel, norm),
        grid=(4,),
        in_specs=[whole(sums), whole(dquery), whole(key_proj), whole(value_proj), weight, weight, weight],
        out_specs=pl.BlockSpec((rows, block), lambda i: (0, i)),
        out_shape=jax.ShapeDtypeStruct((rows, width), jnp.bfloat16),
        scratch_shapes=[pltpu.VMEM((rows, width), jnp.bfloat16)] * 2,
        compiler_params=pltpu.CompilerParams(vmem_limit_bytes=VMEM_LIMIT),
        cost_estimate=pl.CostEstimate(
            flops=2 * rows * width * (3 * width + sums.shape[0]), bytes_accessed=11 << 20, transcendentals=0
        ),
        name="input_grads",
    )(sums, dquery, key_proj, value_proj, w_query, w_key, w_value)


def scatter_sum(part):
    rows, width = part.shape
    plane = lax.axis_size(NEAR)
    depth = lax.axis_size("zh")
    got = lax.all_to_all(part.reshape(plane, rows // plane, width), NEAR, 0, 0)
    mine = jnp.sum(got, axis=0)
    got = lax.all_to_all(mine.reshape(depth, rows // plane // depth, width), "zh", 0, 0)
    return jnp.sum(got, axis=0)


def gather_rows(mine, beside):
    rows, width = mine.shape
    plane = lax.axis_size(NEAR)
    depth = lax.axis_size("zh")
    got = lax.all_to_all(jnp.broadcast_to(mine, (depth, rows, width)), "zh", 0, 0)
    got, beside = lax.optimization_barrier((got.reshape(depth * rows, width), beside))
    got = lax.all_to_all(jnp.broadcast_to(got, (plane, depth * rows, width)), NEAR, 0, 0)
    return got.reshape(plane * depth * rows, width), beside


def scatter_rows(part, axis):
    return lax.psum_scatter(part, axis, scatter_dimension=0, tiled=True)


def keep_half(part, axis):
    if lax.axis_size(axis) == 1:
        return part[0]
    me = lax.axis_index(axis)
    other = lax.dynamic_index_in_dim(part, 1 - me, 0, keepdims=False)
    mine = lax.dynamic_index_in_dim(part, me, 0, keepdims=False)
    return mine + lax.ppermute(other, axis, [(0, 1), (1, 0)])


def pair_sum(part, axis):
    return part + lax.ppermute(part, axis, [(0, 1), (1, 0)])


def body(inputs, w_query, w_key, w_value, key_proj, value_proj, cotangent):
    inputs, cotangent = inputs[0], cotangent[0]
    rows, width = inputs.shape
    proj = key_proj.shape[0]
    n_seq = lax.axis_size(SEQ)
    n_yh = lax.axis_size("yh")
    n_data = lax.axis_size(("yl", "core"))
    norm = 1.0 / math.sqrt(rows * n_seq)
    factor = 1.0 / math.sqrt(rows * n_seq * n_data)

    query, part, inputs_t, seen = project(inputs, w_query, w_key, w_value, key_proj, value_proj)
    seen = scatter_rows(seen.reshape(width, 2 * proj), Z)
    sums, seen = gather_rows(scatter_sum(part), seen)
    sums, seen = lax.optimization_barrier((sums, scatter_rows(seen, "x")))
    seen = keep_half(seen.reshape(n_yh, -1, 2 * proj), "yh")

    attended, dquery, part, other, mine = attend(query, cotangent, sums, inputs_t, norm)

    part, seen = lax.optimization_barrier((part, seen))

    grad_q = mine + lax.ppermute(other, "core", [(0, 1), (1, 0)])
    grad_q = scatter_rows(grad_q.reshape(-1, width // n_data), Z)
    sums, grad_q = gather_rows(scatter_sum(part), grad_q)
    sums, grad_q = lax.optimization_barrier((sums, scatter_rows(grad_q, "x")))
    grad_q = jnp.moveaxis(grad_q.reshape(2, n_yh, -1, width // n_data), 1, 0)
    grad_q = keep_half(grad_q, "yh")
    grad_q = jnp.concatenate([grad_q[0], grad_q[1]], axis=1)

    low = (sums * norm).astype(jnp.bfloat16)
    dkp_low, dvp_low = low[:proj], low[proj:]
    seen_high = seen.astype(jnp.bfloat16)
    seen_low = (seen - seen_high.astype(jnp.float32)).astype(jnp.bfloat16)
    grad_k = dot(seen_high[:, :proj], dkp_low) + dot(seen_low[:, :proj], dkp_low)
    grad_v = dot(seen_high[:, proj:], dvp_low) + dot(seen_low[:, proj:], dvp_low)
    core = lax.axis_index("core")
    grad_q = jnp.concatenate([jnp.where(core == i, grad_q, 0.0) for i in range(2)], axis=1)
    grads = jnp.concatenate([grad_q, grad_k, grad_v], axis=0) * factor
    grads = pair_sum(pair_sum(grads, "core"), "yl")
    grad_q, grad_k, grad_v = jnp.split(grads, 3, axis=0)

    grad_inputs = input_grads(sums, dquery, key_proj, value_proj, w_query, w_key, w_value, norm)
    return (attended[None], grad_inputs[None], grad_q, grad_k, grad_v)


def solution(mesh):
    split = SPLITS[mesh.shape["seq"]]
    fine = Mesh(mesh.devices.reshape((2, 2) + split), ("yl", "core") + SEQ)
    tokens = P(("yl", "core"), SEQ, None)
    return jax.shard_map(
        body,
        mesh=fine,
        in_specs=(tokens, P(), P(), P(), P(None, SEQ), P(None, SEQ), tokens),
        out_specs=(tokens, tokens, P(SEQ, None), P(SEQ, None), P(SEQ, None)),
        check_vma=False,
    )
```

```python
import functools
import math

import jax
import jax.numpy as jnp
from jax import lax
from jax.experimental import pallas as pl
from jax.experimental.pallas import tpu as pltpu
from jax.sharding import Mesh
from jax.sharding import PartitionSpec as P

HEADS = 16
HEAD_DIM = 64
SPLITS = {64: (4, 4, 2, 2), 8: (4, 2, 1, 1)}
SEQ = ("x", "zh", "zl", "yh")
Z = ("zh", "zl")
NEAR = ("x", "yh")
VMEM_LIMIT = 60 * 1024 * 1024
LAST_VMEM = 18 * 1024 * 1024


def dot(a, b):
    return jnp.dot(a, b, preferred_element_type=jnp.float32)


def dot_t(a, b):
    return lax.dot_general(a, b, (((1,), (1,)), ((), ())), preferred_element_type=jnp.float32)


def project_kernel(
    x_ref, wq_ref, wk_ref, wv_ref, kproj_ref, vproj_ref, query_ref, part_ref, xt_ref, seen_ref, projt_ref
):
    width = query_ref.shape[1]
    proj = kproj_ref.shape[0]

    @pl.when(pl.program_id(0) == 0)
    def _():
        projt_ref[:, :proj] = kproj_ref[...].T
        projt_ref[:, proj:] = vproj_ref[...].T

    x = x_ref[...]
    columns = pl.ds(pl.multiple_of(pl.program_id(0) * width, width), width)
    xt = x_ref[:, columns].T
    xt_ref[...] = xt
    n_z, _, chunk, _ = seen_ref.shape
    seen_ref[:, 0] = dot(xt, projt_ref[...]).reshape(n_z, chunk, 2 * proj)
    weights = jnp.concatenate([wk_ref[...], wv_ref[...], wq_ref[...]], axis=1)
    out = dot(x, weights).astype(jnp.bfloat16)
    part_ref[:proj] = dot(kproj_ref[...], out[:, :width])
    part_ref[proj:] = dot(vproj_ref[...], out[:, width : 2 * width])
    query_ref[...] = out[:, 2 * width :]


def project(inputs, w_query, w_key, w_value, key_proj, value_proj):
    rows, width = inputs.shape
    proj = key_proj.shape[0]
    n_x, n_z = lax.axis_size("x"), lax.axis_size(Z)
    block = width // n_x
    whole = lambda a: pl.BlockSpec(a.shape, lambda i: (0, 0))
    weight = pl.BlockSpec((width, block), lambda i: (0, i))
    return pl.pallas_call(
        project_kernel,
        grid=(n_x,),
        in_specs=[whole(inputs), weight, weight, weight, whole(key_proj), whole(value_proj)],
        out_specs=[
            pl.BlockSpec((rows, block), lambda i: (0, i)),
            pl.BlockSpec((2 * proj, block), lambda i: (0, i)),
            pl.BlockSpec((block, rows), lambda i: (i, 0)),
            pl.BlockSpec((n_z, 1, block // n_z, 2 * proj), lambda i: (0, i, 0, 0)),
        ],
        out_shape=[
            jax.ShapeDtypeStruct((rows, width), jnp.bfloat16),
            jax.ShapeDtypeStruct((2 * proj, width), jnp.float32),
            jax.ShapeDtypeStruct((width, rows), jnp.bfloat16),
            jax.ShapeDtypeStruct((n_z, n_x, block // n_z, 2 * proj), jnp.float32),
        ],
        scratch_shapes=[pltpu.VMEM((rows, 2 * proj), jnp.bfloat16)],
        compiler_params=pltpu.CompilerParams(vmem_limit_bytes=VMEM_LIMIT),
        cost_estimate=pl.CostEstimate(
            flops=2 * rows * width * (3 * width + 4 * proj), bytes_accessed=14 << 20, transcendentals=0
        ),
        name="project",
    )(inputs, w_query, w_key, w_value, key_proj, value_proj)


def attend_kernel(
    norm, core_ref, q_ref, c_ref, ks_ref, vs_ref, xt_ref, att_ref, dq_ref, dsum_ref, other_ref, mine_ref
):
    step = pl.program_id(0)
    block = q_ref.shape[1]
    proj = ks_ref.shape[0] * ks_ref.shape[1]
    rows = q_ref.shape[0]
    scale = 1.0 / math.sqrt(HEAD_DIM)
    q, c = q_ref[...], c_ref[...]
    qt, ct = q.T, c.T
    kp32 = (ks_ref[...].reshape(proj, block) * norm).astype(jnp.bfloat16).astype(jnp.float32)
    vp32 = (vs_ref[...].reshape(proj, block) * norm).astype(jnp.bfloat16).astype(jnp.float32)
    kpt = kp32.T.astype(jnp.bfloat16)
    vpt = vp32.T.astype(jnp.bfloat16)
    kps = kp32 * scale
    lane = lax.broadcasted_iota(jnp.int32, (proj, block), 1)
    att, dq = [], []
    dk = dv = None
    for h in range(block // HEAD_DIM):
        mine = (lane >= h * HEAD_DIM) & (lane < (h + 1) * HEAD_DIM)
        sub = slice(h * HEAD_DIM, (h + 1) * HEAD_DIM)
        scores = dot(jnp.where(mine, kps, 0.0).astype(jnp.bfloat16), qt)
        dprob = dot(jnp.where(mine, vp32, 0.0).astype(jnp.bfloat16), ct)
        low, dscore = [], []
        for at in range(0, rows, 128):
            s, d = scores[:, at : at + 128], dprob[:, at : at + 128]
            e = jnp.exp(s - jnp.max(s, axis=0, keepdims=True))
            p = e * (1.0 / jnp.sum(e, axis=0, keepdims=True))
            low.append(p.astype(jnp.bfloat16))
            dscore.append((p * (d - jnp.sum(p * d, axis=0, keepdims=True))).astype(jnp.bfloat16))
        low, dscore = jnp.concatenate(low, axis=1), jnp.concatenate(dscore, axis=1)
        att.append(dot(vpt[sub], low))
        dq.append(dot(kpt[sub], dscore))
        dk_h, dv_h = dot(dscore, q), dot(low, c)
        dk, dv = (dk_h, dv_h) if h == 0 else (jnp.where(mine, dk_h, dk), jnp.where(mine, dv_h, dv))
    att_ref[...] = jnp.concatenate(att, axis=0).T.astype(jnp.bfloat16)
    dquery = (jnp.concatenate(dq, axis=0) * scale).T.astype(jnp.bfloat16)
    dq_ref[...] = dquery
    dsum_ref[:proj] = dk * scale
    dsum_ref[proj:] = dv

    def put(ref):
        n_z, n_x, _, chunk, _ = ref.shape
        for x in range(n_x):
            rows = n_z * chunk
            term = dot(xt_ref[x * rows : (x + 1) * rows], dquery)
            ref[:, x, 0] = term.reshape(n_z, chunk, block)

    pl.when(step < 2)(functools.partial(put, other_ref))
    pl.when(step >= 2)(functools.partial(put, mine_ref))


def attend(query, cotangent, sums, inputs_t, norm, both):
    rows, width = query.shape
    proj = both // 2
    plane = sums.shape[0]
    n_x, n_z = lax.axis_size("x"), lax.axis_size(Z)
    block = width // 4
    core = lax.axis_index("core").astype(jnp.int32).reshape(1)
    place = lambda i, core: lax.rem(i + 2 * (1 - core[0]), 4)
    tokens = pl.BlockSpec((rows, block), lambda i, core: (0, place(i, core)))
    terms = (n_z, n_x, 2, width // (n_x * n_z), block)
    terms_block = (n_z, n_x, 1, width // (n_x * n_z), block)
    return pl.pallas_call(
        functools.partial(attend_kernel, norm),
        grid_spec=pltpu.PrefetchScalarGridSpec(
            num_scalar_prefetch=1,
            grid=(4,),
            in_specs=[
                tokens,
                tokens,
                pl.BlockSpec((plane // 2, both // plane, block), lambda i, core: (0, 0, place(i, core))),
                pl.BlockSpec((plane // 2, both // plane, block), lambda i, core: (1, 0, place(i, core))),
                pl.BlockSpec((width, rows), lambda i, core: (0, 0)),
            ],
            out_specs=[
                tokens,
                tokens,
                pl.BlockSpec((2 * proj, block), lambda i, core: (0, place(i, core))),
                pl.BlockSpec(terms_block, lambda i, core: (0, 0, jnp.minimum(i, 1), 0, 0)),
                pl.BlockSpec(terms_block, lambda i, core: (0, 0, jnp.maximum(i - 2, 0), 0, 0)),
            ],
        ),
        out_shape=[
            jax.ShapeDtypeStruct((rows, width), jnp.bfloat16),
            jax.ShapeDtypeStruct((rows, width), jnp.bfloat16),
            jax.ShapeDtypeStruct((2 * proj, width), jnp.float32),
            jax.ShapeDtypeStruct(terms, jnp.float32),
            jax.ShapeDtypeStruct(terms, jnp.float32),
        ],
        compiler_params=pltpu.CompilerParams(vmem_limit_bytes=VMEM_LIMIT),
        cost_estimate=pl.CostEstimate(
            flops=8 * rows * width * proj * 6, bytes_accessed=12 << 20, transcendentals=rows * HEADS * proj
        ),
        name="attend",
    )(core, query, cotangent, sums, sums, inputs_t)


def input_grads_kernel(
    norm, sums_ref, dq_ref, kproj_ref, vproj_ref, wq_ref, wk_ref, wv_ref, out_ref, dkeys_ref, dvalues_ref
):
    proj = kproj_ref.shape[0]

    @pl.when(pl.program_id(0) == 0)
    def _():
        both = sums_ref[...].reshape(2 * proj, -1) * norm
        dkp = both[:proj].astype(jnp.bfloat16)
        dkeys_ref[...] = dot(kproj_ref[...].T, dkp).astype(jnp.bfloat16)
        dvp = both[proj:].astype(jnp.bfloat16)
        dvalues_ref[...] = dot(vproj_ref[...].T, dvp).astype(jnp.bfloat16)

    grad = dot_t(dq_ref[...], wq_ref[...]) + dot_t(dkeys_ref[...], wk_ref[...])
    out_ref[...] = (grad + dot_t(dvalues_ref[...], wv_ref[...])).astype(jnp.bfloat16)


def input_grads(sums, dquery, key_proj, value_proj, w_query, w_key, w_value, norm):
    rows, width = dquery.shape
    block = width // 4
    plane, both = sums.shape[0], 2 * key_proj.shape[0]
    whole = lambda a: pl.BlockSpec(a.shape, lambda i: (0, 0))
    weight = pl.BlockSpec((block, width), lambda i: (i, 0))
    return pl.pallas_call(
        functools.partial(input_grads_kernel, norm),
        grid=(4,),
        in_specs=[
            pl.BlockSpec((plane, both // plane, width), lambda i: (0, 0, 0)),
            whole(dquery),
            whole(key_proj),
            whole(value_proj),
            weight,
            weight,
            weight,
        ],
        out_specs=pl.BlockSpec((rows, block), lambda i: (0, i)),
        out_shape=jax.ShapeDtypeStruct((rows, width), jnp.bfloat16),
        scratch_shapes=[pltpu.VMEM((rows, width), jnp.bfloat16)] * 2,
        compiler_params=pltpu.CompilerParams(vmem_limit_bytes=LAST_VMEM),
        cost_estimate=pl.CostEstimate(
            flops=2 * rows * width * (3 * width + both), bytes_accessed=11 << 20, transcendentals=0
        ),
        name="input_grads",
    )(sums, dquery, key_proj, value_proj, w_query, w_key, w_value)


def scatter_sum(part):
    rows, width = part.shape
    plane = lax.axis_size(NEAR)
    depth = lax.axis_size(Z)
    got = lax.all_to_all(part.reshape(plane, rows // plane, width), NEAR, 0, 0)
    mine = jnp.sum(got, axis=0)
    got = lax.all_to_all(mine.reshape(depth, rows // plane // depth, width), Z, 0, 0)
    return jnp.sum(got, axis=0)


def gather_rows(mine, extra):
    rows, width = mine.shape
    plane = lax.axis_size(NEAR)
    depth = lax.axis_size(Z)
    got = lax.all_to_all(jnp.broadcast_to(mine, (depth, rows, width)), Z, 0, 0)
    got, extra = lax.optimization_barrier((got.reshape(depth * rows, width), extra))
    got = jnp.broadcast_to(got, (plane, depth * rows, width))
    got = lax.all_to_all(jnp.concatenate([got, extra], axis=1), NEAR, 0, 0)
    return got, jnp.sum(got[:, depth * rows :], axis=0)


def scatter_rows(part, axis):
    return lax.psum_scatter(part, axis, scatter_dimension=0, tiled=True)


def body(inputs, w_query, w_key, w_value, key_proj, value_proj, cotangent):
    inputs, cotangent = inputs[0], cotangent[0]
    rows, width = inputs.shape
    proj = key_proj.shape[0]
    n_seq = lax.axis_size(SEQ)
    n_x, n_yh = lax.axis_size("x"), lax.axis_size("yh")
    n_data = lax.axis_size(("yl", "core"))
    norm = 1.0 / math.sqrt(rows * n_seq)
    factor = 1.0 / math.sqrt(rows * n_seq * n_data)

    query, part, inputs_t, seen = project(inputs, w_query, w_key, w_value, key_proj, value_proj)
    seen = scatter_rows(seen.reshape(width, 2 * proj), Z)
    half = width // n_seq // 2
    seen = jnp.swapaxes(seen.reshape(n_x * n_yh, 2, half, 2 * proj), 1, 2)
    sums, seen = gather_rows(scatter_sum(part), seen.reshape(n_x * n_yh, half, -1))
    seen = jnp.swapaxes(seen.reshape(half, 2, 2 * proj), 0, 1).reshape(-1, 2 * proj)

    attended, dquery, part, other, mine = attend(query, cotangent, sums, inputs_t, norm, 2 * proj)

    grad_q = mine + lax.ppermute(other, "core", [(0, 1), (1, 0)])
    grad_q = scatter_rows(grad_q.reshape(-1, width // n_data), Z)
    grad_q = grad_q.reshape(n_x, 2, n_yh, 2, half, width // n_data).transpose(0, 2, 4, 1, 3, 5)
    sums, grad_q = gather_rows(scatter_sum(part), grad_q.reshape(n_x * n_yh, half, -1))
    grad_q = grad_q.reshape(half, 2, 2, width // n_data).transpose(2, 0, 1, 3).reshape(2 * half, -1)

    low = sums[:, : 2 * proj // (n_x * n_yh)].reshape(2 * proj, width)
    low = (low * norm).astype(jnp.bfloat16)
    dkp_low, dvp_low = low[:proj], low[proj:]
    seen_high = seen.astype(jnp.bfloat16)
    seen_low = (seen - seen_high.astype(jnp.float32)).astype(jnp.bfloat16)
    grad_k = dot(seen_high[:, :proj], dkp_low) + dot(seen_low[:, :proj], dkp_low)
    grad_v = dot(seen_high[:, proj:], dvp_low) + dot(seen_low[:, proj:], dvp_low)
    core = lax.axis_index("core")
    grad_q = jnp.concatenate([jnp.where(core == i, grad_q, 0.0) for i in range(2)], axis=1)
    grads = jnp.concatenate([grad_q, grad_k, grad_v], axis=0) * factor
    across = [lax.ppermute(grads, ("yl", "core"), [(i, i ^ d) for i in range(4)]) for d in (1, 2, 3)]
    grad_inputs = input_grads(sums, dquery, key_proj, value_proj, w_query, w_key, w_value, norm)
    grads = (grads + across[0]) + (across[1] + across[2])
    grad_q, grad_k, grad_v = jnp.split(grads, 3, axis=0)

    return (attended[None], grad_inputs[None], grad_q, grad_k, grad_v)


def solution(mesh):
    split = SPLITS[mesh.shape["seq"]]
    fine = Mesh(mesh.devices.reshape((2, 2) + split), ("yl", "core") + SEQ)
    tokens = P(("yl", "core"), SEQ, None)
    return jax.shard_map(
        body,
        mesh=fine,
        in_specs=(tokens, P(), P(), P(), P(None, SEQ), P(None, SEQ), tokens),
        out_specs=(tokens, tokens, P(SEQ, None), P(SEQ, None), P(SEQ, None)),
        check_vma=False,
    )
```

```python
import functools
import math

import jax
import jax.numpy as jnp
from jax import lax
from jax.experimental import pallas as pl
from jax.experimental.pallas import tpu as pltpu
from jax.sharding import Mesh
from jax.sharding import PartitionSpec as P

HEADS = 16
HEAD_DIM = 64
SPLITS = {64: (4, 4, 2, 2), 8: (4, 2, 1, 1)}
SEQ = ("x", "zh", "zl", "yh")
Z = ("zh", "zl")
NEAR = ("x", "yh")
VMEM_LIMIT = 60 * 1024 * 1024


def dot(a, b):
    return jnp.dot(a, b, preferred_element_type=jnp.float32)


def dot_t(a, b):
    return lax.dot_general(a, b, (((1,), (1,)), ((), ())), preferred_element_type=jnp.float32)


def project_kernel(
    x_ref, wq_ref, wk_ref, wv_ref, kproj_ref, vproj_ref, query_ref, part_ref, xt_ref, seen_ref, projt_ref
):
    width = query_ref.shape[1]
    proj = kproj_ref.shape[0]

    @pl.when(pl.program_id(0) == 0)
    def _():
        projt_ref[:, :proj] = kproj_ref[...].T
        projt_ref[:, proj:] = vproj_ref[...].T

    x = x_ref[...]
    columns = pl.ds(pl.multiple_of(pl.program_id(0) * width, width), width)
    xt = x_ref[:, columns].T
    xt_ref[...] = xt
    n_z, _, chunk, _ = seen_ref.shape
    seen_ref[:, 0] = dot(xt, projt_ref[...]).reshape(n_z, chunk, 2 * proj)
    weights = jnp.concatenate([wk_ref[...], wv_ref[...], wq_ref[...]], axis=1)
    out = dot(x, weights).astype(jnp.bfloat16)
    part_ref[:proj] = dot(kproj_ref[...], out[:, :width])
    part_ref[proj:] = dot(vproj_ref[...], out[:, width : 2 * width])
    query_ref[...] = out[:, 2 * width :]


def project(inputs, w_query, w_key, w_value, key_proj, value_proj):
    rows, width = inputs.shape
    proj = key_proj.shape[0]
    n_x, n_z = lax.axis_size("x"), lax.axis_size(Z)
    block = width // n_x
    whole = lambda a: pl.BlockSpec(a.shape, lambda i: (0, 0))
    weight = pl.BlockSpec((width, block), lambda i: (0, i))
    return pl.pallas_call(
        project_kernel,
        grid=(n_x,),
        in_specs=[whole(inputs), weight, weight, weight, whole(key_proj), whole(value_proj)],
        out_specs=[
            pl.BlockSpec((rows, block), lambda i: (0, i)),
            pl.BlockSpec((2 * proj, block), lambda i: (0, i)),
            pl.BlockSpec((block, rows), lambda i: (i, 0)),
            pl.BlockSpec((n_z, 1, block // n_z, 2 * proj), lambda i: (0, i, 0, 0)),
        ],
        out_shape=[
            jax.ShapeDtypeStruct((rows, width), jnp.bfloat16),
            jax.ShapeDtypeStruct((2 * proj, width), jnp.float32),
            jax.ShapeDtypeStruct((width, rows), jnp.bfloat16),
            jax.ShapeDtypeStruct((n_z, n_x, block // n_z, 2 * proj), jnp.float32),
        ],
        scratch_shapes=[pltpu.VMEM((rows, 2 * proj), jnp.bfloat16)],
        compiler_params=pltpu.CompilerParams(vmem_limit_bytes=VMEM_LIMIT),
        cost_estimate=pl.CostEstimate(
            flops=2 * rows * width * (3 * width + 4 * proj), bytes_accessed=14 << 20, transcendentals=0
        ),
        name="project",
    )(inputs, w_query, w_key, w_value, key_proj, value_proj)


def attend_kernel(
    norm, core_ref, q_ref, c_ref, ks_ref, vs_ref, xt_ref, att_ref, dq_ref, dsum_ref, other_ref, mine_ref
):
    step = pl.program_id(0)
    block = q_ref.shape[1]
    proj = ks_ref.shape[0] * ks_ref.shape[1]
    rows = q_ref.shape[0]
    scale = 1.0 / math.sqrt(HEAD_DIM)
    q, c = q_ref[...], c_ref[...]
    qt, ct = q.T, c.T
    kp32 = (ks_ref[...].reshape(proj, block) * norm).astype(jnp.bfloat16).astype(jnp.float32)
    vp32 = (vs_ref[...].reshape(proj, block) * norm).astype(jnp.bfloat16).astype(jnp.float32)
    kpt = kp32.T.astype(jnp.bfloat16)
    vpt = vp32.T.astype(jnp.bfloat16)
    kps = kp32 * scale
    lane = lax.broadcasted_iota(jnp.int32, (proj, block), 1)
    att, dq = [], []
    dk = dv = None
    for h in range(block // HEAD_DIM):
        mine = (lane >= h * HEAD_DIM) & (lane < (h + 1) * HEAD_DIM)
        sub = slice(h * HEAD_DIM, (h + 1) * HEAD_DIM)
        scores = dot(jnp.where(mine, kps, 0.0).astype(jnp.bfloat16), qt)
        dprob = dot(jnp.where(mine, vp32, 0.0).astype(jnp.bfloat16), ct)
        low, dscore = [], []
        for at in range(0, rows, 128):
            s, d = scores[:, at : at + 128], dprob[:, at : at + 128]
            e = jnp.exp(s - jnp.max(s, axis=0, keepdims=True))
            p = e * (1.0 / jnp.sum(e, axis=0, keepdims=True))
            low.append(p.astype(jnp.bfloat16))
            dscore.append((p * (d - jnp.sum(p * d, axis=0, keepdims=True))).astype(jnp.bfloat16))
        low, dscore = jnp.concatenate(low, axis=1), jnp.concatenate(dscore, axis=1)
        att.append(dot(vpt[sub], low))
        dq.append(dot(kpt[sub], dscore))
        dk_h, dv_h = dot(dscore, q), dot(low, c)
        dk, dv = (dk_h, dv_h) if h == 0 else (jnp.where(mine, dk_h, dk), jnp.where(mine, dv_h, dv))
    att_ref[...] = jnp.concatenate(att, axis=0).T.astype(jnp.bfloat16)
    dquery = (jnp.concatenate(dq, axis=0) * scale).T.astype(jnp.bfloat16)
    dq_ref[...] = dquery
    dsum_ref[:proj] = dk * scale
    dsum_ref[proj:] = dv

    def put(ref):
        n_z, n_x, _, chunk, _ = ref.shape
        for x in range(n_x):
            rows = n_z * chunk
            term = dot(xt_ref[x * rows : (x + 1) * rows], dquery)
            ref[:, x, 0] = term.reshape(n_z, chunk, block)

    pl.when(step < 2)(functools.partial(put, other_ref))
    pl.when(step >= 2)(functools.partial(put, mine_ref))


def attend(query, cotangent, sums, inputs_t, norm, both):
    rows, width = query.shape
    proj = both // 2
    plane = sums.shape[0]
    n_x, n_z = lax.axis_size("x"), lax.axis_size(Z)
    block = width // 4
    core = lax.axis_index("core").astype(jnp.int32).reshape(1)
    place = lambda i, core: lax.rem(i + 2 * (1 - core[0]), 4)
    tokens = pl.BlockSpec((rows, block), lambda i, core: (0, place(i, core)))
    terms = (n_z, n_x, 2, width // (n_x * n_z), block)
    terms_block = (n_z, n_x, 1, width // (n_x * n_z), block)
    return pl.pallas_call(
        functools.partial(attend_kernel, norm),
        grid_spec=pltpu.PrefetchScalarGridSpec(
            num_scalar_prefetch=1,
            grid=(4,),
            in_specs=[
                tokens,
                tokens,
                pl.BlockSpec((plane // 2, both // plane, block), lambda i, core: (0, 0, place(i, core))),
                pl.BlockSpec((plane // 2, both // plane, block), lambda i, core: (1, 0, place(i, core))),
                pl.BlockSpec((width, rows), lambda i, core: (0, 0)),
            ],
            out_specs=[
                tokens,
                tokens,
                pl.BlockSpec((2 * proj, block), lambda i, core: (0, place(i, core))),
                pl.BlockSpec(terms_block, lambda i, core: (0, 0, jnp.minimum(i, 1), 0, 0)),
                pl.BlockSpec(terms_block, lambda i, core: (0, 0, jnp.maximum(i - 2, 0), 0, 0)),
            ],
        ),
        out_shape=[
            jax.ShapeDtypeStruct((rows, width), jnp.bfloat16),
            jax.ShapeDtypeStruct((rows, width), jnp.bfloat16),
            jax.ShapeDtypeStruct((2 * proj, width), jnp.float32),
            jax.ShapeDtypeStruct(terms, jnp.float32),
            jax.ShapeDtypeStruct(terms, jnp.float32),
        ],
        compiler_params=pltpu.CompilerParams(vmem_limit_bytes=VMEM_LIMIT),
        cost_estimate=pl.CostEstimate(
            flops=8 * rows * width * proj * 6, bytes_accessed=12 << 20, transcendentals=rows * HEADS * proj
        ),
        name="attend",
    )(core, query, cotangent, sums, sums, inputs_t)


def input_grads_kernel(
    norm, sums_ref, dq_ref, kproj_ref, vproj_ref, wq_ref, wk_ref, wv_ref, out_ref, dkeys_ref, dvalues_ref
):
    proj = kproj_ref.shape[0]

    @pl.when(pl.program_id(0) == 0)
    def _():
        both = sums_ref[...].reshape(2 * proj, -1) * norm
        dkp = both[:proj].astype(jnp.bfloat16)
        dkeys_ref[...] = dot(kproj_ref[...].T, dkp).astype(jnp.bfloat16)
        dvp = both[proj:].astype(jnp.bfloat16)
        dvalues_ref[...] = dot(vproj_ref[...].T, dvp).astype(jnp.bfloat16)

    grad = dot_t(dq_ref[...], wq_ref[...]) + dot_t(dkeys_ref[...], wk_ref[...])
    out_ref[...] = (grad + dot_t(dvalues_ref[...], wv_ref[...])).astype(jnp.bfloat16)


def input_grads(sums, dquery, key_proj, value_proj, w_query, w_key, w_value, norm):
    rows, width = dquery.shape
    block = width // 4
    plane, both = sums.shape[0], 2 * key_proj.shape[0]
    whole = lambda a: pl.BlockSpec(a.shape, lambda i: (0, 0))
    weight = pl.BlockSpec((block, width), lambda i: (i, 0))
    return pl.pallas_call(
        functools.partial(input_grads_kernel, norm),
        grid=(4,),
        in_specs=[
            pl.BlockSpec((plane, both // plane, width), lambda i: (0, 0, 0)),
            whole(dquery),
            whole(key_proj),
            whole(value_proj),
            weight,
            weight,
            weight,
        ],
        out_specs=pl.BlockSpec((rows, block), lambda i: (0, i)),
        out_shape=jax.ShapeDtypeStruct((rows, width), jnp.bfloat16),
        scratch_shapes=[pltpu.VMEM((rows, width), jnp.bfloat16)] * 2,
        compiler_params=pltpu.CompilerParams(vmem_limit_bytes=VMEM_LIMIT),
        cost_estimate=pl.CostEstimate(
            flops=2 * rows * width * (3 * width + both), bytes_accessed=11 << 20, transcendentals=0
        ),
        name="input_grads",
    )(sums, dquery, key_proj, value_proj, w_query, w_key, w_value)


def scatter_sum(part):
    rows, width = part.shape
    plane = lax.axis_size(NEAR)
    depth = lax.axis_size(Z)
    got = lax.all_to_all(part.reshape(plane, rows // plane, width), NEAR, 0, 0)
    mine = jnp.sum(got, axis=0)
    got = lax.all_to_all(mine.reshape(depth, rows // plane // depth, width), Z, 0, 0)
    return jnp.sum(got, axis=0)


def gather_rows(mine, extra):
    rows, width = mine.shape
    plane = lax.axis_size(NEAR)
    depth = lax.axis_size(Z)
    got = lax.all_to_all(jnp.broadcast_to(mine, (depth, rows, width)), Z, 0, 0)
    got, extra = lax.optimization_barrier((got.reshape(depth * rows, width), extra))
    got = jnp.broadcast_to(got, (plane, depth * rows, width))
    got = lax.all_to_all(jnp.concatenate([got, extra], axis=1), NEAR, 0, 0)
    return got, jnp.sum(got[:, depth * rows :], axis=0)


def scatter_rows(part, axis):
    return lax.psum_scatter(part, axis, scatter_dimension=0, tiled=True)


def body(inputs, w_query, w_key, w_value, key_proj, value_proj, cotangent):
    inputs, cotangent = inputs[0], cotangent[0]
    rows, width = inputs.shape
    proj = key_proj.shape[0]
    n_seq = lax.axis_size(SEQ)
    n_x, n_yh = lax.axis_size("x"), lax.axis_size("yh")
    n_data = lax.axis_size(("yl", "core"))
    norm = 1.0 / math.sqrt(rows * n_seq)
    factor = 1.0 / math.sqrt(rows * n_seq * n_data)

    query, part, inputs_t, seen = project(inputs, w_query, w_key, w_value, key_proj, value_proj)
    seen = scatter_rows(seen.reshape(width, 2 * proj), Z)
    half = width // n_seq // 2
    seen = jnp.swapaxes(seen.reshape(n_x * n_yh, 2, half, 2 * proj), 1, 2)
    sums, seen = gather_rows(scatter_sum(part), seen.reshape(n_x * n_yh, half, -1))
    seen = jnp.swapaxes(seen.reshape(half, 2, 2 * proj), 0, 1).reshape(-1, 2 * proj)

    attended, dquery, part, other, mine = attend(query, cotangent, sums, inputs_t, norm, 2 * proj)

    grad_q = mine + lax.ppermute(other, "core", [(0, 1), (1, 0)])
    grad_q = scatter_rows(grad_q.reshape(-1, width // n_data), Z)
    grad_q = grad_q.reshape(n_x, 2, n_yh, 2, half, width // n_data).transpose(0, 2, 4, 1, 3, 5)
    sums, grad_q = gather_rows(scatter_sum(part), grad_q.reshape(n_x * n_yh, half, -1))
    grad_q = grad_q.reshape(half, 2, 2, width // n_data).transpose(2, 0, 1, 3).reshape(2 * half, -1)

    low = sums[:, : 2 * proj // (n_x * n_yh)].reshape(2 * proj, width)
    low = (low * norm).astype(jnp.bfloat16)
    dkp_low, dvp_low = low[:proj], low[proj:]
    seen_high = seen.astype(jnp.bfloat16)
    seen_low = (seen - seen_high.astype(jnp.float32)).astype(jnp.bfloat16)
    grad_k = dot(seen_high[:, :proj], dkp_low) + dot(seen_low[:, :proj], dkp_low)
    grad_v = dot(seen_high[:, proj:], dvp_low) + dot(seen_low[:, proj:], dvp_low)
    core = lax.axis_index("core")
    grad_q = jnp.concatenate([jnp.where(core == i, grad_q, 0.0) for i in range(2)], axis=1)
    grads = jnp.concatenate([grad_q, grad_k, grad_v], axis=0) * factor
    across = [lax.ppermute(grads, ("yl", "core"), [(i, i ^ d) for i in range(4)]) for d in (1, 2, 3)]
    grad_inputs = input_grads(sums, dquery, key_proj, value_proj, w_query, w_key, w_value, norm)
    grads = (grads + across[0]) + (across[1] + across[2])
    grad_q, grad_k, grad_v = jnp.split(grads, 3, axis=0)

    return (attended[None], grad_inputs[None], grad_q, grad_k, grad_v)


def solution(mesh):
    split = SPLITS[mesh.shape["seq"]]
    fine = Mesh(mesh.devices.reshape((2, 2) + split), ("yl", "core") + SEQ)
    tokens = P(("yl", "core"), SEQ, None)
    return jax.shard_map(
        body,
        mesh=fine,
        in_specs=(tokens, P(), P(), P(), P(None, SEQ), P(None, SEQ), tokens),
        out_specs=(tokens, tokens, P(SEQ, None), P(SEQ, None), P(SEQ, None)),
        check_vma=False,
    )
```

```python
import functools
import math

import jax
import jax.numpy as jnp
from jax import lax
from jax.experimental import pallas as pl
from jax.experimental.pallas import tpu as pltpu
from jax.sharding import Mesh
from jax.sharding import PartitionSpec as P

HEADS = 16
HEAD_DIM = 64
SPLITS = {64: (4, 4, 2, 2), 8: (4, 2, 1, 1)}
SEQ = ("x", "zh", "zl", "yh")
Z = ("zh", "zl")
NEAR = ("x", "yh")
VMEM_LIMIT = 60 * 1024 * 1024


def dot(a, b):
    return jnp.dot(a, b, preferred_element_type=jnp.float32)


def dot_t(a, b):
    return lax.dot_general(a, b, (((1,), (1,)), ((), ())), preferred_element_type=jnp.float32)


def project_kernel(
    x_ref, wq_ref, wk_ref, wv_ref, kproj_ref, vproj_ref, query_ref, part_ref, xt_ref, seen_ref, projt_ref
):
    width = query_ref.shape[1]
    proj = kproj_ref.shape[0]

    @pl.when(pl.program_id(0) == 0)
    def _():
        projt_ref[:, :proj] = kproj_ref[...].T
        projt_ref[:, proj:] = vproj_ref[...].T

    x = x_ref[...]
    columns = pl.ds(pl.multiple_of(pl.program_id(0) * width, width), width)
    xt = x_ref[:, columns].T
    xt_ref[...] = xt
    n_z, _, chunk, _ = seen_ref.shape
    seen_ref[:, 0] = dot(xt, projt_ref[...]).reshape(n_z, chunk, 2 * proj)
    weights = jnp.concatenate([wk_ref[...], wv_ref[...], wq_ref[...]], axis=1)
    out = dot(x, weights).astype(jnp.bfloat16)
    part_ref[:proj] = dot(kproj_ref[...], out[:, :width])
    part_ref[proj:] = dot(vproj_ref[...], out[:, width : 2 * width])
    query_ref[...] = out[:, 2 * width :]


def project(inputs, w_query, w_key, w_value, key_proj, value_proj):
    rows, width = inputs.shape
    proj = key_proj.shape[0]
    n_x, n_z = lax.axis_size("x"), lax.axis_size(Z)
    block = width // n_x
    whole = lambda a: pl.BlockSpec(a.shape, lambda i: (0, 0))
    weight = pl.BlockSpec((width, block), lambda i: (0, i))
    return pl.pallas_call(
        project_kernel,
        grid=(n_x,),
        in_specs=[whole(inputs), weight, weight, weight, whole(key_proj), whole(value_proj)],
        out_specs=[
            pl.BlockSpec((rows, block), lambda i: (0, i)),
            pl.BlockSpec((2 * proj, block), lambda i: (0, i)),
            pl.BlockSpec((block, rows), lambda i: (i, 0)),
            pl.BlockSpec((n_z, 1, block // n_z, 2 * proj), lambda i: (0, i, 0, 0)),
        ],
        out_shape=[
            jax.ShapeDtypeStruct((rows, width), jnp.bfloat16),
            jax.ShapeDtypeStruct((2 * proj, width), jnp.float32),
            jax.ShapeDtypeStruct((width, rows), jnp.bfloat16),
            jax.ShapeDtypeStruct((n_z, n_x, block // n_z, 2 * proj), jnp.float32),
        ],
        scratch_shapes=[pltpu.VMEM((rows, 2 * proj), jnp.bfloat16)],
        compiler_params=pltpu.CompilerParams(vmem_limit_bytes=VMEM_LIMIT),
        cost_estimate=pl.CostEstimate(
            flops=2 * rows * width * (3 * width + 4 * proj), bytes_accessed=14 << 20, transcendentals=0
        ),
        name="project",
    )(inputs, w_query, w_key, w_value, key_proj, value_proj)


def attend_kernel(
    norm, core_ref, q_ref, c_ref, ks_ref, vs_ref, xt_ref, att_ref, dq_ref, dsum_ref, other_ref, mine_ref
):
    step = pl.program_id(0)
    block = q_ref.shape[1]
    proj = ks_ref.shape[0] * ks_ref.shape[1]
    rows = q_ref.shape[0]
    scale = 1.0 / math.sqrt(HEAD_DIM)
    q, c = q_ref[...], c_ref[...]
    qt, ct = q.T, c.T
    kp32 = (ks_ref[...].reshape(proj, block) * norm).astype(jnp.bfloat16).astype(jnp.float32)
    vp32 = (vs_ref[...].reshape(proj, block) * norm).astype(jnp.bfloat16).astype(jnp.float32)
    kpt = kp32.T.astype(jnp.bfloat16)
    vpt = vp32.T.astype(jnp.bfloat16)
    kps = kp32 * scale
    lane = lax.broadcasted_iota(jnp.int32, (proj, block), 1)
    att, dq = [], []
    dk = dv = None
    for h in range(block // HEAD_DIM):
        mine = (lane >= h * HEAD_DIM) & (lane < (h + 1) * HEAD_DIM)
        sub = slice(h * HEAD_DIM, (h + 1) * HEAD_DIM)
        scores = dot(jnp.where(mine, kps, 0.0).astype(jnp.bfloat16), qt)
        dprob = dot(jnp.where(mine, vp32, 0.0).astype(jnp.bfloat16), ct)
        low, dscore = [], []
        for at in range(0, rows, 128):
            s, d = scores[:, at : at + 128], dprob[:, at : at + 128]
            e = jnp.exp(s - jnp.max(s, axis=0, keepdims=True))
            p = e * (1.0 / jnp.sum(e, axis=0, keepdims=True))
            low.append(p.astype(jnp.bfloat16))
            dscore.append((p * (d - jnp.sum(p * d, axis=0, keepdims=True))).astype(jnp.bfloat16))
        low, dscore = jnp.concatenate(low, axis=1), jnp.concatenate(dscore, axis=1)
        att.append(dot(vpt[sub], low))
        dq.append(dot(kpt[sub], dscore))
        dk_h, dv_h = dot(dscore, q), dot(low, c)
        dk, dv = (dk_h, dv_h) if h == 0 else (jnp.where(mine, dk_h, dk), jnp.where(mine, dv_h, dv))
    att_ref[...] = jnp.concatenate(att, axis=0).T.astype(jnp.bfloat16)
    dquery = (jnp.concatenate(dq, axis=0) * scale).T.astype(jnp.bfloat16)
    dq_ref[...] = dquery
    dsum_ref[:proj] = dk * scale
    dsum_ref[proj:] = dv

    def put(ref):
        n_z, n_x, _, chunk, _ = ref.shape
        for x in range(n_x):
            rows = n_z * chunk
            term = dot(xt_ref[x * rows : (x + 1) * rows], dquery)
            ref[:, x, 0] = term.reshape(n_z, chunk, block)

    pl.when(step < 2)(functools.partial(put, other_ref))
    pl.when(step >= 2)(functools.partial(put, mine_ref))


def attend(query, cotangent, sums, inputs_t, norm, both):
    rows, width = query.shape
    proj = both // 2
    plane = sums.shape[0]
    n_x, n_z = lax.axis_size("x"), lax.axis_size(Z)
    block = width // 4
    core = lax.axis_index("core").astype(jnp.int32).reshape(1)
    place = lambda i, core: lax.rem(i + 2 * (1 - core[0]), 4)
    tokens = pl.BlockSpec((rows, block), lambda i, core: (0, place(i, core)))
    terms = (n_z, n_x, 2, width // (n_x * n_z), block)
    terms_block = (n_z, n_x, 1, width // (n_x * n_z), block)
    return pl.pallas_call(
        functools.partial(attend_kernel, norm),
        grid_spec=pltpu.PrefetchScalarGridSpec(
            num_scalar_prefetch=1,
            grid=(4,),
            in_specs=[
                tokens,
                tokens,
                pl.BlockSpec((plane // 2, both // plane, block), lambda i, core: (0, 0, place(i, core))),
                pl.BlockSpec((plane // 2, both // plane, block), lambda i, core: (1, 0, place(i, core))),
                pl.BlockSpec((width, rows), lambda i, core: (0, 0)),
            ],
            out_specs=[
                tokens,
                tokens,
                pl.BlockSpec((2 * proj, block), lambda i, core: (0, place(i, core))),
                pl.BlockSpec(terms_block, lambda i, core: (0, 0, jnp.minimum(i, 1), 0, 0)),
                pl.BlockSpec(terms_block, lambda i, core: (0, 0, jnp.maximum(i - 2, 0), 0, 0)),
            ],
        ),
        out_shape=[
            jax.ShapeDtypeStruct((rows, width), jnp.bfloat16),
            jax.ShapeDtypeStruct((rows, width), jnp.bfloat16),
            jax.ShapeDtypeStruct((2 * proj, width), jnp.float32),
            jax.ShapeDtypeStruct(terms, jnp.float32),
            jax.ShapeDtypeStruct(terms, jnp.float32),
        ],
        compiler_params=pltpu.CompilerParams(vmem_limit_bytes=VMEM_LIMIT - 3 * 1024 * 1024),
        cost_estimate=pl.CostEstimate(
            flops=8 * rows * width * proj * 6, bytes_accessed=12 << 20, transcendentals=rows * HEADS * proj
        ),
        name="attend",
    )(core, query, cotangent, sums, sums, inputs_t)


def input_grads_kernel(
    norm, sums_ref, dq_ref, kproj_ref, vproj_ref, wq_ref, wk_ref, wv_ref, out_ref, dkeys_ref, dvalues_ref
):
    proj = kproj_ref.shape[0]

    @pl.when(pl.program_id(0) == 0)
    def _():
        both = sums_ref[...].reshape(2 * proj, -1) * norm
        dkp = both[:proj].astype(jnp.bfloat16)
        dkeys_ref[...] = dot(kproj_ref[...].T, dkp).astype(jnp.bfloat16)
        dvp = both[proj:].astype(jnp.bfloat16)
        dvalues_ref[...] = dot(vproj_ref[...].T, dvp).astype(jnp.bfloat16)

    grad = dot_t(dq_ref[...], wq_ref[...]) + dot_t(dkeys_ref[...], wk_ref[...])
    out_ref[...] = (grad + dot_t(dvalues_ref[...], wv_ref[...])).astype(jnp.bfloat16)


def input_grads(sums, dquery, key_proj, value_proj, w_query, w_key, w_value, norm):
    rows, width = dquery.shape
    block = width // 4
    plane, both = sums.shape[0], 2 * key_proj.shape[0]
    whole = lambda a: pl.BlockSpec(a.shape, lambda i: (0, 0))
    weight = pl.BlockSpec((block, width), lambda i: (i, 0))
    return pl.pallas_call(
        functools.partial(input_grads_kernel, norm),
        grid=(4,),
        in_specs=[
            pl.BlockSpec((plane, both // plane, width), lambda i: (0, 0, 0)),
            whole(dquery),
            whole(key_proj),
            whole(value_proj),
            weight,
            weight,
            weight,
        ],
        out_specs=pl.BlockSpec((rows, block), lambda i: (0, i)),
        out_shape=jax.ShapeDtypeStruct((rows, width), jnp.bfloat16),
        scratch_shapes=[pltpu.VMEM((rows, width), jnp.bfloat16)] * 2,
        compiler_params=pltpu.CompilerParams(vmem_limit_bytes=VMEM_LIMIT),
        cost_estimate=pl.CostEstimate(
            flops=2 * rows * width * (3 * width + both), bytes_accessed=11 << 20, transcendentals=0
        ),
        name="input_grads",
    )(sums, dquery, key_proj, value_proj, w_query, w_key, w_value)


def scatter_sum(part):
    rows, width = part.shape
    plane = lax.axis_size(NEAR)
    depth = lax.axis_size(Z)
    got = lax.all_to_all(part.reshape(plane, rows // plane, width), NEAR, 0, 0)
    mine = jnp.sum(got, axis=0)
    got = lax.all_to_all(mine.reshape(depth, rows // plane // depth, width), Z, 0, 0)
    return jnp.sum(got, axis=0)


def gather_rows(mine, extra):
    rows, width = mine.shape
    plane = lax.axis_size(NEAR)
    depth = lax.axis_size(Z)
    got = lax.all_to_all(jnp.broadcast_to(mine, (depth, rows, width)), Z, 0, 0)
    got, extra = lax.optimization_barrier((got.reshape(depth * rows, width), extra))
    got = jnp.broadcast_to(got, (plane, depth * rows, width))
    got = lax.all_to_all(jnp.concatenate([got, extra], axis=1), NEAR, 0, 0)
    return got, jnp.sum(got[:, depth * rows :], axis=0)


def scatter_rows(part, axis):
    return lax.psum_scatter(part, axis, scatter_dimension=0, tiled=True)


def body(inputs, w_query, w_key, w_value, key_proj, value_proj, cotangent):
    inputs, cotangent = inputs[0], cotangent[0]
    rows, width = inputs.shape
    proj = key_proj.shape[0]
    n_seq = lax.axis_size(SEQ)
    n_x, n_yh = lax.axis_size("x"), lax.axis_size("yh")
    n_data = lax.axis_size(("yl", "core"))
    norm = 1.0 / math.sqrt(rows * n_seq)
    factor = 1.0 / math.sqrt(rows * n_seq * n_data)

    query, part, inputs_t, seen = project(inputs, w_query, w_key, w_value, key_proj, value_proj)
    seen = scatter_rows(seen.reshape(width, 2 * proj), Z)
    half = width // n_seq // 2
    seen = jnp.swapaxes(seen.reshape(n_x * n_yh, 2, half, 2 * proj), 1, 2)
    sums, seen = gather_rows(scatter_sum(part), seen.reshape(n_x * n_yh, half, -1))
    seen = jnp.swapaxes(seen.reshape(half, 2, 2 * proj), 0, 1).reshape(-1, 2 * proj)

    attended, dquery, part, other, mine = attend(query, cotangent, sums, inputs_t, norm, 2 * proj)

    grad_q = mine + lax.ppermute(other, "core", [(0, 1), (1, 0)])
    grad_q = scatter_rows(grad_q.reshape(-1, width // n_data), Z)
    grad_q = grad_q.reshape(n_x, 2, n_yh, 2, half, width // n_data).transpose(0, 2, 4, 1, 3, 5)
    sums, grad_q = gather_rows(scatter_sum(part), grad_q.reshape(n_x * n_yh, half, -1))
    grad_q = grad_q.reshape(half, 2, 2, width // n_data).transpose(2, 0, 1, 3).reshape(2 * half, -1)

    low = sums[:, : 2 * proj // (n_x * n_yh)].reshape(2 * proj, width)
    low = (low * norm).astype(jnp.bfloat16)
    dkp_low, dvp_low = low[:proj], low[proj:]
    seen_high = seen.astype(jnp.bfloat16)
    seen_low = (seen - seen_high.astype(jnp.float32)).astype(jnp.bfloat16)
    grad_k = dot(seen_high[:, :proj], dkp_low) + dot(seen_low[:, :proj], dkp_low)
    grad_v = dot(seen_high[:, proj:], dvp_low) + dot(seen_low[:, proj:], dvp_low)
    core = lax.axis_index("core")
    grad_q = jnp.concatenate([jnp.where(core == i, grad_q, 0.0) for i in range(2)], axis=1)
    grads = jnp.concatenate([grad_q, grad_k, grad_v], axis=0) * factor
    across = [lax.ppermute(grads, ("yl", "core"), [(i, i ^ d) for i in range(4)]) for d in (1, 2, 3)]
    grad_inputs = input_grads(sums, dquery, key_proj, value_proj, w_query, w_key, w_value, norm)
    grads = (grads + across[0]) + (across[1] + across[2])
    grad_q, grad_k, grad_v = jnp.split(grads, 3, axis=0)

    return (attended[None], grad_inputs[None], grad_q, grad_k, grad_v)


def solution(mesh):
    split = SPLITS[mesh.shape["seq"]]
    fine = Mesh(mesh.devices.reshape((2, 2) + split), ("yl", "core") + SEQ)
    tokens = P(("yl", "core"), SEQ, None)
    return jax.shard_map(
        body,
        mesh=fine,
        in_specs=(tokens, P(), P(), P(), P(None, SEQ), P(None, SEQ), tokens),
        out_specs=(tokens, tokens, P(SEQ, None), P(SEQ, None), P(SEQ, None)),
        check_vma=False,
    )
```
